32 devices in a mesh: grp: 2 (over y), srv: 16 (over z, x, core).
Axes of the slice: x: 2, y: 2, z: 4, core: 2. Of those that a mesh axis runs over, the one named last changes fastest.
Arguments:
- queries: bfloat16 [12288, 1536], P(('grp', 'srv')), parts along dimension 0, may hold values from -4096 to 4096
- latent_rope: bfloat16 [12288, 576], P(('grp', 'srv')), parts along dimension 0, may hold values from -16 to 16
- doc_start: int32 [12288], P(('grp', 'srv')), parts along dimension 0, may hold values from 0 to 6143, as said below
- w_kv_up: bfloat16 [512, 2048], replicated, may hold values from -0.25 to 0.25
- w_out: bfloat16 [1024, 2048], replicated, may hold values from -0.5 to 0.5
Outputs:
- mixed: bfloat16 [12288, 2048], P(('grp', 'srv')), parts along dimension 0
The draws below stay inside these ranges and needn't reach their ends.
There are 2 independent parts, one for each index of `grp`. The reference program is written for one: setup_inputs(seed, part) draws one part's arguments, and reference() takes and returns one part's arrays. A program takes and returns all parts, laid end to end along the dimension named above; an argument that names none is the same for every part. Nothing has to cross between parts.
Inputs may be any that keep to these rules, and one draw needn't show every extreme that they name: doc_start[i] <= i < doc_start[i] + 2688; doc_start[i] is i or doc_start[i-1]; the first document has exactly 2688 positions.
All inputs are finite; a program needn't handle non-finite values.
Results may differ from the reference program's by a relative error of at most 0.0063.
Values may be sent and summed in bfloat16 or wider, within the bound.
A program may use at most 128 MiB of HBM per device.

```python
import math
import jax
import jax.numpy as jnp
from jax import lax

D = 2048
H = 8
DN = 128
DR = 64
DV = 128
R = 512
TOK_DEV = 384
REACH = 7
TOKENS = 6144
DOCMAX = 2688


def draw_common(key):
    latent = jax.random.normal(jax.random.fold_in(key, 101), (TOKENS, R + DR), jnp.float32)
    query_all = jax.random.normal(jax.random.fold_in(key, 202), (TOKENS, H, DN + DR), jnp.float32)
    return (latent, query_all)


def draw_queries(key, part):
    latent, query_all = draw_common(key)
    return query_all.reshape(TOKENS, H * (DN + DR)).astype(jnp.bfloat16)


def draw_latent_rope(key, part):
    latent, query_all = draw_common(key)
    return latent.astype(jnp.bfloat16)


def draw_doc_start(key, part):
    lengths = jax.random.randint(jax.random.fold_in(key, 404), (TOKENS,), 1, DOCMAX + 1).astype(jnp.int32)
    lengths = lengths.at[0].set(DOCMAX)
    starts = (jnp.cumsum(lengths) - lengths).astype(jnp.int32)
    positions = jnp.arange(TOKENS, dtype=jnp.int32)
    doc_index = (jnp.searchsorted(starts, positions, side='right') - 1).astype(jnp.int32)
    return starts[doc_index].astype(jnp.int32)


def centred(rng, dims, width, bound, kind=jnp.bfloat16):
    values = width * jax.random.normal(rng, dims, jnp.float32)
    return jnp.clip(values, min=-bound, max=bound).astype(kind)


def setup_inputs(seed: int = 0, part: int = 0) -> dict:
    keys = jax.random.split(jax.random.key(seed), 6)
    own_keys = jax.random.split(jax.random.fold_in(keys[5], part), 6)
    return {
        "queries": draw_queries(jax.random.fold_in(jax.random.fold_in(keys[5], part), 71), part),
        "latent_rope": draw_latent_rope(jax.random.fold_in(jax.random.fold_in(keys[5], part), 71), part),
        "doc_start": draw_doc_start(jax.random.fold_in(jax.random.fold_in(keys[5], part), 71), part),
        "w_kv_up": centred(keys[3], (R, H * (DN + DV)), R ** -0.5, 0.25),
        "w_out": centred(keys[4], (H * DV, D), DV ** -0.5, 0.5),
    }


def block_terms(query_nope, query_rope, key_nope, values, key_rope, query_pos, key_pos, starts):
    score_scale = 1.0 / math.sqrt(DN + DR)
    scores = jnp.einsum('ihc,jhc->hij', query_nope.astype(jnp.float32), key_nope.astype(jnp.float32))
    scores = scores + jnp.einsum('ihc,jc->hij', query_rope.astype(jnp.float32), key_rope.astype(jnp.float32))
    scores = scores * score_scale
    allowed = (key_pos[None, :] >= starts[:, None]) & (key_pos[None, :] <= query_pos[:, None])
    masked = jnp.where(allowed[None], scores, -jnp.inf)
    block_max = jnp.maximum(lax.optimization_barrier(jnp.max(masked, axis=2)), jnp.float32(-1e+30))
    weights = jnp.where(allowed[None], jnp.exp(scores - block_max[:, :, None]), jnp.float32(0.0))
    block_total = lax.optimization_barrier(jnp.sum(weights, axis=2))
    rounded = lax.optimization_barrier(weights.astype(jnp.bfloat16))
    block_out = jnp.einsum('hij,jhc->ihc', rounded.astype(jnp.float32), values.astype(jnp.float32))
    return (block_out, block_max, block_total)

def merge_blocks(pieces):
    top_max = pieces[0][1]
    for block_part in pieces[1:]:
        top_max = jnp.maximum(top_max, block_part[1])
    numerator = jnp.zeros(pieces[0][0].shape, jnp.float32)
    denominator = jnp.zeros(pieces[0][0].shape[:2] + (1,), jnp.float32)
    for block_part in pieces:
        factor = jnp.exp(block_part[1] - top_max)
        numerator = numerator + factor.T[:, :, None] * block_part[0]
        denominator = denominator + (factor * block_part[2]).T[:, :, None]
    return (numerator / denominator).astype(jnp.bfloat16)

def reference(queries, latent_rope, doc_start, w_kv_up, w_out):
    blocks = TOKENS // TOK_DEV
    keys_values = jnp.dot(latent_rope[:, :R], w_kv_up, preferred_element_type=jnp.float32).astype(jnp.bfloat16)
    keys_values = keys_values.reshape(blocks, TOK_DEV, H, DN + DV)
    key_ropes = latent_rope[:, R:].reshape(blocks, TOK_DEV, DR)
    query_blocks = queries.reshape(blocks, TOK_DEV, H, DN + DR)
    start_blocks = doc_start.reshape(blocks, TOK_DEV)
    offsets = jnp.arange(TOK_DEV, dtype=jnp.int32)

    def attend_block(block_index):
        query_here = query_blocks[block_index]
        starts = start_blocks[block_index]
        query_pos = block_index * TOK_DEV + offsets
        pieces = []
        for distance in range(REACH + 1):
            source = jnp.maximum(block_index - distance, 0).astype(jnp.int32)
            key_kv = keys_values[source]
            key_pos = query_pos - distance * TOK_DEV
            pieces.append(block_terms(query_here[:, :, :DN], query_here[:, :, DN:], key_kv[:, :, :DN], key_kv[:, :, DN:], key_ropes[source], query_pos, key_pos, starts))
        return merge_blocks(pieces)
    attended = lax.map(attend_block, jnp.arange(blocks, dtype=jnp.int32))
    attended = attended.reshape(TOKENS, H * DV)
    return jnp.dot(attended, w_out, preferred_element_type=jnp.float32).astype(jnp.bfloat16)
```

```python
import functools
import math

import jax
import jax.numpy as jnp
from jax import lax
from jax.experimental import pallas as pl
from jax.experimental.pallas import tpu as pltpu
from jax.sharding import PartitionSpec as P

DN = 128
DR = 64
DV = 128
R = 512
REACH = 7
DQ = DN + DR
PARTS = 3
NEG = -1e30
MESH = pl.DeviceIdType.MESH

ORDER = ((4, 3, 7, 2, 1, 5, 6), (1, 4, 5, 2, 3, 6, 7), (2, 1, 4, 3, 7, 6, 5), (1, 2, 3, 4, 5, 6, 7))
TAKE = (
    ((4,), (3,), (7,), (2,), (1,), (5,), (6,)),
    ((1,), (4,), (5,), (2,), (3,), (6,), (7,)),
    ((2, 4), (1,), (), (3, 7), (6,), (), (5,)),
    ((1,), (2, 4), (3,), (), (6, 5), (), (7,)),
)


def kernel(n, heads, q_hbm, lat_hbm, start_hbm, wkv_hbm, wout_hbm, o_hbm,
           held, q_in, q_s, lat_in, start_in, start_s, wkv, wout, rope, acc, top, att, out,
           in_sem, out_sem, send_sem, recv_sem):
    rows = q_in.shape[0]
    part = rows // PARTS
    extra = part * DR // R
    me = lax.axis_index("srv")
    z, x, c = me // 4, (me // 2) % 2, me % 2
    depth = n // 4
    place = 2 * x + c
    scale = math.log2(math.e) / math.sqrt(DQ)

    loads = [
        pltpu.make_async_copy(a, b, in_sem.at[i])
        for i, (a, b) in enumerate(
            ((lat_hbm, lat_in), (q_hbm, q_in), (start_hbm, start_in), (wkv_hbm, wkv), (wout_hbm, wout))
        )
    ]
    for load in loads:
        load.start()

    has_next = z + 1 < depth
    middle = jnp.logical_and(z >= 1, has_next)
    partners = (
        (1 - 2 * c, True),
        (2 - 4 * x, True),
        (4, has_next),
        (-4, z >= 1),
        (3, jnp.logical_and(c == 1, middle)),
        (-3, jnp.logical_and(c == 0, z >= 2)),
    )
    barrier = pltpu.get_barrier_semaphore()
    for delta, cond in partners:
        def greet(delta=delta):
            pl.semaphore_signal(barrier, inc=1, device_id={"srv": me + delta}, device_id_type=MESH)
        greet() if cond is True else pl.when(cond)(greet)

    corner = jnp.logical_and(x == 0, c == 0)
    sends = (
        (0, 1, c == 0),
        (0, 2, x == 0),
        (0, 4, has_next),
        (2, 1 - 2 * c, me >= 2),
        (2, 4, jnp.logical_and(corner, middle)),
        (4, 1 - 2 * c, z >= 1),
        (4, 2 - 4 * x, z >= 1),
        (4, 3, jnp.logical_and(c == 1, middle)),
        (5, 1, jnp.logical_and(corner, z >= 2)),
        (6, 1 - 2 * c, jnp.logical_and(me >= 6, jnp.logical_or(x == 1, c == 0))),
        (7, -2, jnp.logical_and(jnp.logical_and(x == 1, c == 0), me >= 7)),
    )

    def remote(i, k):
        d, delta, _ = sends[i]
        return pltpu.make_async_remote_copy(
            src_ref=held.at[d, k],
            dst_ref=held.at[d + delta, k],
            send_sem=send_sem.at[i, k],
            recv_sem=recv_sem.at[d + delta, k],
            device_id={"srv": me + delta},
            device_id_type=MESH,
        )

    def pass_on(d, k):
        for i, (source, _, cond) in enumerate(sends):
            if source == d:
                pl.when(cond)(lambda i=i: remote(i, k).start())

    def take(distances):
        for k in range(PARTS):
            for d in distances:
                @pl.when(d <= me)
                def _(d=d):
                    pltpu.make_async_remote_copy(
                        src_ref=held.at[d, k],
                        dst_ref=held.at[d, k],
                        send_sem=send_sem.at[0, k],
                        recv_sem=recv_sem.at[d, k],
                        device_id={"srv": me + 1 - 2 * c},
                        device_id_type=MESH,
                    ).wait_recv()
                    pass_on(d, k)

    count = 2 + has_next.astype(jnp.int32) + (z >= 1).astype(jnp.int32)
    count = count + jnp.logical_and(c == 1, middle).astype(jnp.int32)
    count = count + jnp.logical_and(c == 0, z >= 2).astype(jnp.int32)

    loads[0].wait()
    for k in range(PARTS):
        held[0, k, :part, :] = lat_in[k * part:(k + 1) * part, :R]
        held[0, k, part:, :] = jnp.concatenate(
            [lat_in[k * part + g * extra:k * part + (g + 1) * extra, R:] for g in range(R // DR)], axis=1
        )
    pl.semaphore_wait(barrier, count)
    for k in range(PARTS):
        pass_on(0, k)

    loads[1].wait()
    for h in range(heads):
        q_s[h] = q_in[:, h * DQ:(h + 1) * DQ]
    loads[2].wait()
    starts = jnp.broadcast_to(start_in[...].astype(jnp.float32), (128, rows))
    start_s[...] = jnp.transpose(starts).astype(jnp.int32)
    loads[3].wait()

    def block(d, own):
        for k in range(PARTS):
            for g in range(R // DR):
                rope[k * part + g * extra:k * part + (g + 1) * extra, :] = held[
                    d, k, part:, g * DR:(g + 1) * DR
                ]
        first = start_s[...] - (me - d) * rows
        first = jnp.concatenate([first] * (rows // 128), axis=1)
        ones = jnp.ones((rows, 128), jnp.bfloat16)

        def one(h):
            latent = held[d, :, :part, :].reshape(rows, R)
            columns = pl.ds(pl.multiple_of(h * (DN + DV), DN + DV), DN + DV)
            kv = jnp.dot(latent, wkv[:, columns], preferred_element_type=jnp.float32).astype(jnp.bfloat16)
            keys = jnp.concatenate([kv[:, :DN], rope[...]], axis=1)
            values = jnp.concatenate([kv[:, DN:], ones], axis=1)
            s = lax.dot_general(
                q_s[h], keys, (((1,), (1,)), ((), ())), preferred_element_type=jnp.float32
            )
            position = lax.broadcasted_iota(jnp.int32, (rows, rows), 1)
            allowed = position >= first
            if own:
                row = lax.broadcasted_iota(jnp.int32, (rows, rows), 0)
                allowed = jnp.logical_and(allowed, position <= row)
            s = jnp.where(allowed, s, NEG)
            best = jnp.max(s, axis=1, keepdims=True)
            if own:
                new = jnp.broadcast_to(best, (rows, 128))
            else:
                old = top[h]
                new = jnp.maximum(old, best)
            p = jnp.exp2((s - jnp.concatenate([new] * (rows // 128), axis=1)) * scale)
            pv = jnp.dot(p.astype(jnp.bfloat16), values, preferred_element_type=jnp.float32)
            if own:
                acc[h] = pv
            else:
                factor = jnp.exp2((old - new) * scale)
                acc[h] = acc[h] * jnp.concatenate([factor, factor], axis=1) + pv
            top[h] = new

        @pl.loop(0, heads // 2)
        def _(pair):
            one(2 * pair)
            one(2 * pair + 1)

    block(0, True)

    def digits(order):
        return sum(d * 8**i for i, d in enumerate(order))

    codes = [digits(order) for order in ORDER]
    code = (
        (1 - x) * (1 - c) * codes[0] + (1 - x) * c * codes[1] + x * (1 - c) * codes[2] + x * c * codes[3]
    )

    def step(t, code):
        for i in range(REACH):
            for p in range(4):
                if TAKE[p][i]:
                    @pl.when(jnp.logical_and(t == i, place == p))
                    def _(p=p, i=i):
                        take(TAKE[p][i])
        d = code % 8
        pl.when(d <= me)(lambda: block(d, False))
        return code // 8

    lax.fori_loop(0, REACH, step, code)

    for h in range(heads):
        att[:, h * DV:(h + 1) * DV] = (acc[h, :, :DV] / acc[h, :, DV:]).astype(jnp.bfloat16)
    loads[4].wait()
    width = wout.shape[1]
    tile = 512
    tiles = width // tile

    def store(i):
        at = pl.ds(i * tile, tile)
        return pltpu.make_async_copy(out.at[:, at], o_hbm.at[:, at], out_sem.at[i])

    for i in range(tiles):
        out[:, i * tile:(i + 1) * tile] = jnp.dot(
            att[...], wout[:, i * tile:(i + 1) * tile], preferred_element_type=jnp.float32
        ).astype(jnp.bfloat16)
        store(i).start()
    for i in range(len(sends)):
        @pl.when(sends[i][2])
        def _(i=i):
            for k in range(PARTS):
                remote(i, k).wait_send()
    for i in range(tiles):
        store(i).wait()


def local(n, queries, latent_rope, doc_start, w_kv_up, w_out):
    rows = queries.shape[0]
    heads = w_out.shape[0] // DV
    part = rows // PARTS
    sends = 11
    bf, f32 = jnp.bfloat16, jnp.float32
    return pl.pallas_call(
        functools.partial(kernel, n, heads),
        out_shape=jax.ShapeDtypeStruct((rows, w_out.shape[1]), bf),
        in_specs=[pl.BlockSpec(memory_space=pl.ANY)] * 5,
        out_specs=pl.BlockSpec(memory_space=pl.ANY),
        scratch_shapes=[
            pltpu.VMEM((REACH + 1, PARTS, part + part * DR // R, R), bf),
            pltpu.VMEM(queries.shape, bf),
            pltpu.VMEM((heads, rows, DQ), bf),
            pltpu.VMEM(latent_rope.shape, bf),
            pltpu.VMEM((1, rows), jnp.int32),
            pltpu.VMEM((rows, 128), jnp.int32),
            pltpu.VMEM(w_kv_up.shape, bf),
            pltpu.VMEM(w_out.shape, bf),
            pltpu.VMEM((rows, DR), bf),
            pltpu.VMEM((heads, rows, 2 * DV), f32),
            pltpu.VMEM((heads, rows, 128), f32),
            pltpu.VMEM((rows, heads * DV), bf),
            pltpu.VMEM((rows, w_out.shape[1]), bf),
            pltpu.SemaphoreType.DMA((5,)),
            pltpu.SemaphoreType.DMA((4,)),
            pltpu.SemaphoreType.DMA((sends, PARTS)),
            pltpu.SemaphoreType.DMA((REACH + 1, PARTS)),
        ],
        compiler_params=pltpu.CompilerParams(
            collective_id=0, has_side_effects=True, vmem_limit_bytes=48 * 1024 * 1024
        ),
        cost_estimate=pl.CostEstimate(
            flops=20 * 10**9, bytes_accessed=10**7, transcendentals=8 * heads * rows * rows
        ),
    )(queries, latent_rope, doc_start.reshape(1, rows), w_kv_up, w_out)


def solution(mesh):
    in_specs = (P(("grp", "srv"), None), P(("grp", "srv"), None), P(("grp", "srv")), P(), P())
    out_specs = P(("grp", "srv"), None)
    return jax.shard_map(
        functools.partial(local, mesh.shape["srv"]), mesh=mesh, in_specs=in_specs, out_specs=out_specs,
        check_vma=False,
    )
```

```python
import functools
import math

import jax
import jax.numpy as jnp
from jax import lax
from jax.experimental import pallas as pl
from jax.experimental.pallas import tpu as pltpu
from jax.sharding import PartitionSpec as P

DN = 128
DR = 64
DV = 128
R = 512
REACH = 7
DQ = DN + DR
PARTS = 3
GROUP = 2
NEG = -1e30
MESH = pl.DeviceIdType.MESH

ORDER = ((4, 3, 7, 2, 1, 5, 6), (1, 4, 5, 2, 3, 6, 7), (2, 1, 4, 3, 7, 6, 5), (1, 2, 3, 4, 5, 6, 7))
TAKE = (
    ((4,), (3,), (7,), (2,), (1,), (5,), (6,)),
    ((1,), (4,), (5,), (2,), (3,), (6,), (7,)),
    ((2, 4), (1,), (), (3, 7), (6,), (), (5,)),
    ((1,), (2, 4), (3,), (), (6, 5), (), (7,)),
)


def kernel(n, heads, q_hbm, lat_hbm, start_hbm, wkv_hbm, wout_hbm, o_hbm,
           held, q_in, q_s, start_in, wk, wv, wvt, wout, lat, bias, acc, top, att, out,
           lat_sem, in_sem, w_sem, out_sem, send_sem, recv_sem):
    rows = q_in.shape[0]
    part = rows // PARTS
    me = lax.axis_index("srv")
    z, x, c = me // 4, (me // 2) % 2, me % 2
    depth = n // 4
    place = 2 * x + c
    scale = math.log2(math.e) / math.sqrt(DQ)

    own_loads = [
        pltpu.make_async_copy(lat_hbm.at[:, pl.ds(k * part, part)], held.at[0, k], lat_sem.at[k])
        for k in range(PARTS)
    ]
    loads = [
        pltpu.make_async_copy(a, b, in_sem.at[i])
        for i, (a, b) in enumerate(((start_hbm, start_in), (q_hbm, q_in), (wout_hbm, wout)))
    ]
    w_loads = [
        pltpu.make_async_copy(
            wkv_hbm.at[:, pl.ds(h * (DN + DV) + i * DN, DN)], b.at[:, pl.ds(h * DN, DN)], w_sem.at[i, h]
        )
        for i, b in ((0, wk), (1, wv))
        for h in range(heads)
    ]
    for load in own_loads + loads[:2] + w_loads + loads[2:]:
        load.start()

    has_next = z + 1 < depth
    middle = jnp.logical_and(z >= 1, has_next)
    partners = (
        (1 - 2 * c, True),
        (2 - 4 * x, True),
        (4, has_next),
        (-4, z >= 1),
        (3, jnp.logical_and(c == 1, middle)),
        (-3, jnp.logical_and(c == 0, z >= 2)),
    )
    barrier = pltpu.get_barrier_semaphore()
    for delta, cond in partners:
        def greet(delta=delta):
            pl.semaphore_signal(barrier, inc=1, device_id={"srv": me + delta}, device_id_type=MESH)
        greet() if cond is True else pl.when(cond)(greet)

    corner = jnp.logical_and(x == 0, c == 0)
    sends = (
        (0, 1, c == 0),
        (0, 2, x == 0),
        (0, 4, has_next),
        (2, 1 - 2 * c, me >= 2),
        (2, 4, jnp.logical_and(corner, middle)),
        (4, 1 - 2 * c, z >= 1),
        (4, 2 - 4 * x, z >= 1),
        (4, 3, jnp.logical_and(c == 1, middle)),
        (5, 1, jnp.logical_and(corner, z >= 2)),
        (6, 1 - 2 * c, jnp.logical_and(me >= 6, jnp.logical_or(x == 1, c == 0))),
        (7, -2, jnp.logical_and(jnp.logical_and(x == 1, c == 0), me >= 7)),
    )

    def remote(i, k):
        d, delta, _ = sends[i]
        return pltpu.make_async_remote_copy(
            src_ref=held.at[d, k],
            dst_ref=held.at[d + delta, k],
            send_sem=send_sem.at[i, k],
            recv_sem=recv_sem.at[d + delta, k],
            device_id={"srv": me + delta},
            device_id_type=MESH,
        )

    def pass_on(d, k):
        for i, (source, _, cond) in enumerate(sends):
            if source == d:
                pl.when(cond)(lambda i=i: remote(i, k).start())

    def take(distances):
        for k in range(PARTS):
            for d in distances:
                @pl.when(d <= me)
                def _(d=d):
                    pltpu.make_async_remote_copy(
                        src_ref=held.at[d, k],
                        dst_ref=held.at[d, k],
                        send_sem=send_sem.at[0, k],
                        recv_sem=recv_sem.at[d, k],
                        device_id={"srv": me + 1 - 2 * c},
                        device_id_type=MESH,
                    ).wait_recv()
                    pass_on(d, k)

    count = 2 + has_next.astype(jnp.int32) + (z >= 1).astype(jnp.int32)
    count = count + jnp.logical_and(c == 1, middle).astype(jnp.int32)
    count = count + jnp.logical_and(c == 0, z >= 2).astype(jnp.int32)

    for load in own_loads:
        load.wait()
    pl.semaphore_wait(barrier, count)
    for k in range(PARTS):
        pass_on(0, k)

    loads[1].wait()
    for h in range(heads):
        q_s[h] = jnp.transpose(q_in[:, h * DQ:(h + 1) * DQ])
    for load in w_loads:
        load.wait()
    for h in range(heads):
        wvt[h * DV:(h + 1) * DV, :] = jnp.transpose(wv[:, h * DV:(h + 1) * DV])
    loads[0].wait()

    def block(d, own):
        for k in range(PARTS):
            lat[k * part:(k + 1) * part, :] = jnp.transpose(held[d, k])
        first = start_in[...].reshape(1, rows) - (me - d) * rows
        position = lax.broadcasted_iota(jnp.int32, (rows, rows), 0)
        allowed = position >= first
        if own:
            allowed = jnp.logical_and(allowed, position <= lax.broadcasted_iota(jnp.int32, (rows, rows), 1))
        bias[...] = jnp.where(allowed, jnp.float32(0.0), jnp.float32(NEG))
        ones = jnp.ones((16, rows), jnp.bfloat16)

        def one(h, k_nope, values):
            keys = jnp.concatenate([k_nope, lat[:, R:]], axis=1)
            s = jnp.dot(keys, q_s[h], preferred_element_type=jnp.float32) + bias[...]
            new = jnp.max(s, axis=0, keepdims=True)
            if not own:
                old = top[h]
                new = jnp.maximum(old, new)
            p = jnp.exp2((s - new) * scale)
            values = jnp.concatenate([values, ones], axis=0)
            pv = jnp.dot(values, p.astype(jnp.bfloat16), preferred_element_type=jnp.float32)
            if own:
                acc[h] = pv
            else:
                acc[h] = acc[h] * jnp.exp2((old - new) * scale) + pv
            top[h] = new

        @pl.loop(0, heads // GROUP)
        def _(group):
            at = pl.ds(pl.multiple_of(group * GROUP * DN, GROUP * DN), GROUP * DN)
            latent_t = jnp.concatenate([held[d, k, :R, :] for k in range(PARTS)], axis=1)
            k_nope = jnp.dot(lat[:, :R], wk[:, at], preferred_element_type=jnp.float32)
            k_nope = k_nope.astype(jnp.bfloat16)
            values = jnp.dot(wvt[at, :], latent_t, preferred_element_type=jnp.float32)
            values = values.astype(jnp.bfloat16)
            for i in range(GROUP):
                one(group * GROUP + i, k_nope[:, i * DN:(i + 1) * DN], values[i * DV:(i + 1) * DV, :])

    block(0, True)

    def digits(order):
        return sum(d * 8**i for i, d in enumerate(order))

    codes = [digits(order) for order in ORDER]
    code = (
        (1 - x) * (1 - c) * codes[0] + (1 - x) * c * codes[1] + x * (1 - c) * codes[2] + x * c * codes[3]
    )

    def step(t, code):
        for i in range(REACH):
            for p in range(4):
                if TAKE[p][i]:
                    @pl.when(jnp.logical_and(t == i, place == p))
                    def _(p=p, i=i):
                        take(TAKE[p][i])
        d = code % 8
        pl.when(d <= me)(lambda: block(d, False))
        return code // 8

    lax.fori_loop(0, REACH, step, code)

    for h in range(heads):
        attended = acc[h, :DV, :] / acc[h, DV:DV + 1, :]
        att[:, h * DV:(h + 1) * DV] = jnp.transpose(attended.astype(jnp.bfloat16))
    loads[2].wait()
    width = wout.shape[1]
    tile = 512
    tiles = width // tile

    def store(i):
        at = pl.ds(i * tile, tile)
        return pltpu.make_async_copy(out.at[:, at], o_hbm.at[:, at], out_sem.at[i])

    for i in range(tiles):
        out[:, i * tile:(i + 1) * tile] = jnp.dot(
            att[...], wout[:, i * tile:(i + 1) * tile], preferred_element_type=jnp.float32
        ).astype(jnp.bfloat16)
        store(i).start()
    for i in range(len(sends)):
        @pl.when(sends[i][2])
        def _(i=i):
            for k in range(PARTS):
                remote(i, k).wait_send()
    for i in range(tiles):
        store(i).wait()


def local(n, queries, latent_rope, doc_start, w_kv_up, w_out):
    rows = queries.shape[0]
    heads = w_out.shape[0] // DV
    part = rows // PARTS
    sends = 11
    bf, f32 = jnp.bfloat16, jnp.float32
    return pl.pallas_call(
        functools.partial(kernel, n, heads),
        out_shape=jax.ShapeDtypeStruct((rows, w_out.shape[1]), bf),
        in_specs=[pl.BlockSpec(memory_space=pltpu.HBM)] * 5,
        out_specs=pl.BlockSpec(memory_space=pltpu.HBM),
        scratch_shapes=[
            pltpu.VMEM((REACH + 1, PARTS, R + DR, part), bf),
            pltpu.VMEM(queries.shape, bf),
            pltpu.VMEM((heads, DQ, rows), bf),
            pltpu.VMEM(doc_start.shape, jnp.int32),
            pltpu.VMEM((R, heads * DN), bf),
            pltpu.VMEM((R, heads * DV), bf),
            pltpu.VMEM((heads * DV, R), bf),
            pltpu.VMEM(w_out.shape, bf),
            pltpu.VMEM(latent_rope.shape, bf),
            pltpu.VMEM((rows, rows), f32),
            pltpu.VMEM((heads, DV + 16, rows), f32),
            pltpu.VMEM((heads, 1, rows), f32),
            pltpu.VMEM((rows, heads * DV), bf),
            pltpu.VMEM((rows, w_out.shape[1]), bf),
            pltpu.SemaphoreType.DMA((PARTS,)),
            pltpu.SemaphoreType.DMA((3,)),
            pltpu.SemaphoreType.DMA((2, heads)),
            pltpu.SemaphoreType.DMA((4,)),
            pltpu.SemaphoreType.DMA((sends, PARTS)),
            pltpu.SemaphoreType.DMA((REACH + 1, PARTS)),
        ],
        compiler_params=pltpu.CompilerParams(
            collective_id=0, has_side_effects=True, vmem_limit_bytes=48 * 1024 * 1024
        ),
        cost_estimate=pl.CostEstimate(
            flops=20 * 10**9, bytes_accessed=10**7, transcendentals=8 * heads * rows * rows
        ),
    )(queries, latent_rope.T, doc_start, w_kv_up, w_out)


def solution(mesh):
    in_specs = (P(("grp", "srv"), None), P(("grp", "srv"), None), P(("grp", "srv")), P(), P())
    out_specs = P(("grp", "srv"), None)
    return jax.shard_map(
        functools.partial(local, mesh.shape["srv"]), mesh=mesh, in_specs=in_specs, out_specs=out_specs,
        check_vma=False,
    )
```

```python
import functools
import math

import jax
import jax.numpy as jnp
from jax import lax
from jax.experimental import pallas as pl
from jax.experimental.pallas import tpu as pltpu
from jax.sharding import PartitionSpec as P

DN = 128
DR = 64
DV = 128
R = 512
REACH = 7
DQ = DN + DR
PARTS = 3
NEG = -1e30
MESH = pl.DeviceIdType.MESH

ORDER = ((4, 3, 7, 2, 1, 5, 6), (1, 4, 5, 2, 3, 6, 7), (2, 1, 4, 3, 7, 6, 5), (1, 2, 3, 4, 5, 6, 7))
TAKE = (
    ((4,), (3,), (7,), (2,), (1,), (5,), (6,)),
    ((1,), (4,), (5,), (2,), (3,), (6,), (7,)),
    ((2, 4), (1,), (), (3, 7), (6,), (), (5,)),
    ((1,), (2, 4), (3,), (), (6, 5), (), (7,)),
)


def kernel(n, heads, q_hbm, lat_hbm, start_hbm, wkv_hbm, wout_hbm, o_hbm,
           held, q_in, q_s, start_in, wk, wv, wvt, wout, lat, bias, acc, top, att, out,
           lat_sem, in_sem, w_sem, out_sem, send_sem, recv_sem):
    rows = q_in.shape[0]
    part = rows // PARTS
    me = lax.axis_index("srv")
    z, x, c = me // 4, (me // 2) % 2, me % 2
    depth = n // 4
    place = 2 * x + c
    scale = math.log2(math.e) / math.sqrt(DQ)

    own_loads = [
        pltpu.make_async_copy(lat_hbm.at[:, pl.ds(k * part, part)], held.at[0, k], lat_sem.at[k])
        for k in range(PARTS)
    ]
    loads = [
        pltpu.make_async_copy(a, b, in_sem.at[i])
        for i, (a, b) in enumerate(((start_hbm, start_in), (q_hbm, q_in), (wout_hbm, wout)))
    ]
    w_loads = [
        pltpu.make_async_copy(
            wkv_hbm.at[:, pl.ds(h * (DN + DV) + i * DN, DN)], b.at[:, pl.ds(h * DN, DN)], w_sem.at[i, h]
        )
        for i, b in ((0, wk), (1, wv))
        for h in range(heads)
    ]
    for load in own_loads + loads[:2] + w_loads + loads[2:]:
        load.start()

    has_next = z + 1 < depth
    middle = jnp.logical_and(z >= 1, has_next)
    partners = (
        (1 - 2 * c, True),
        (2 - 4 * x, True),
        (4, has_next),
        (-4, z >= 1),
        (3, jnp.logical_and(c == 1, middle)),
        (-3, jnp.logical_and(c == 0, z >= 2)),
    )
    barrier = pltpu.get_barrier_semaphore()
    for delta, cond in partners:
        def greet(delta=delta):
            pl.semaphore_signal(barrier, inc=1, device_id={"srv": me + delta}, device_id_type=MESH)
        greet() if cond is True else pl.when(cond)(greet)

    corner = jnp.logical_and(x == 0, c == 0)
    sends = (
        (0, 1, c == 0),
        (0, 2, x == 0),
        (0, 4, has_next),
        (2, 1 - 2 * c, me >= 2),
        (2, 4, jnp.logical_and(corner, middle)),
        (4, 1 - 2 * c, z >= 1),
        (4, 2 - 4 * x, z >= 1),
        (4, 3, jnp.logical_and(c == 1, middle)),
        (5, 1, jnp.logical_and(corner, z >= 2)),
        (6, 1 - 2 * c, jnp.logical_and(me >= 6, jnp.logical_or(x == 1, c == 0))),
        (7, -2, jnp.logical_and(jnp.logical_and(x == 1, c == 0), me >= 7)),
    )

    def remote(i, k):
        d, delta, _ = sends[i]
        return pltpu.make_async_remote_copy(
            src_ref=held.at[d, k],
            dst_ref=held.at[d + delta, k],
            send_sem=send_sem.at[i, k],
            recv_sem=recv_sem.at[d + delta, k],
            device_id={"srv": me + delta},
            device_id_type=MESH,
        )

    def pass_on(d, k):
        for i, (source, _, cond) in enumerate(sends):
            if source == d:
                pl.when(cond)(lambda i=i: remote(i, k).start())

    def take(distances):
        for k in range(PARTS):
            for d in distances:
                @pl.when(d <= me)
                def _(d=d):
                    pltpu.make_async_remote_copy(
                        src_ref=held.at[d, k],
                        dst_ref=held.at[d, k],
                        send_sem=send_sem.at[0, k],
                        recv_sem=recv_sem.at[d, k],
                        device_id={"srv": me + 1 - 2 * c},
                        device_id_type=MESH,
                    ).wait_recv()
                    pass_on(d, k)

    count = 2 + has_next.astype(jnp.int32) + (z >= 1).astype(jnp.int32)
    count = count + jnp.logical_and(c == 1, middle).astype(jnp.int32)
    count = count + jnp.logical_and(c == 0, z >= 2).astype(jnp.int32)

    for load in own_loads:
        load.wait()
    pl.semaphore_wait(barrier, count)
    for k in range(PARTS):
        pass_on(0, k)

    loads[1].wait()
    for h in range(heads):
        q_s[h] = jnp.transpose(q_in[:, h * DQ:(h + 1) * DQ])
    for load in w_loads:
        load.wait()
    for h in range(heads):
        wvt[h * DV:(h + 1) * DV, :] = jnp.transpose(wv[:, h * DV:(h + 1) * DV])
    loads[0].wait()

    def block(d, own):
        for k in range(PARTS):
            lat[k * part:(k + 1) * part, :] = jnp.transpose(held[d, k])
        first = start_in[...].reshape(1, rows) - (me - d) * rows
        position = lax.broadcasted_iota(jnp.int32, (rows, rows), 0)
        allowed = position >= first
        if own:
            allowed = jnp.logical_and(allowed, position <= lax.broadcasted_iota(jnp.int32, (rows, rows), 1))
        bias[...] = jnp.where(allowed, jnp.float32(0.0), jnp.float32(NEG))
        ones = jnp.ones((16, rows), jnp.bfloat16)

        latent_t = jnp.concatenate([held[d, k, :R, :] for k in range(PARTS)], axis=1)

        def expand(pair):
            at = slice(pair * 2 * DN, (pair + 1) * 2 * DN)
            k_nope = jnp.dot(lat[:, :R], wk[:, at], preferred_element_type=jnp.float32)
            values = jnp.dot(wvt[at, :], latent_t, preferred_element_type=jnp.float32)
            return k_nope.astype(jnp.bfloat16), values.astype(jnp.bfloat16)

        def score(h, pair):
            i = h % 2
            keys = jnp.concatenate([pair[0][:, i * DN:(i + 1) * DN], lat[:, R:]], axis=1)
            return jnp.dot(keys, q_s[h], preferred_element_type=jnp.float32)

        def weigh(h, s):
            s = s + bias[...]
            new = jnp.max(s, axis=0, keepdims=True)
            factor = None
            if not own:
                old = top[h]
                new = jnp.maximum(old, new)
                factor = jnp.exp2((old - new) * scale)
            top[h] = new
            return jnp.exp2((s - new) * scale).astype(jnp.bfloat16), factor

        def add(h, pair, p, factor):
            i = h % 2
            values = jnp.concatenate([pair[1][i * DV:(i + 1) * DV, :], ones], axis=0)
            pv = jnp.dot(values, p, preferred_element_type=jnp.float32)
            acc[h] = pv if own else acc[h] * factor + pv

        pairs = {0: expand(0)}
        scores = {0: score(0, pairs[0])}
        for h in range(heads):
            if h + 1 < heads:
                scores[h + 1] = score(h + 1, pairs[(h + 1) // 2])
            if h % 2 == 0 and h + 2 < heads:
                pairs[h // 2 + 1] = expand(h // 2 + 1)
            add(h, pairs[h // 2], *weigh(h, scores.pop(h)))

    block(0, True)

    def digits(order):
        return sum(d * 8**i for i, d in enumerate(order))

    codes = [digits(order) for order in ORDER]
    code = (
        (1 - x) * (1 - c) * codes[0] + (1 - x) * c * codes[1] + x * (1 - c) * codes[2] + x * c * codes[3]
    )

    def step(t, code):
        for i in range(REACH):
            for p in range(4):
                if TAKE[p][i]:
                    @pl.when(jnp.logical_and(t == i, place == p))
                    def _(p=p, i=i):
                        take(TAKE[p][i])
        d = code % 8
        pl.when(d <= me)(lambda: block(d, False))
        return code // 8

    lax.fori_loop(0, REACH, step, code)

    for h in range(heads):
        attended = acc[h, :DV, :] / acc[h, DV:DV + 1, :]
        att[:, h * DV:(h + 1) * DV] = jnp.transpose(attended.astype(jnp.bfloat16))
    loads[2].wait()
    width = wout.shape[1]
    tile = 512
    tiles = width // tile

    def store(i):
        at = pl.ds(i * tile, tile)
        return pltpu.make_async_copy(out.at[:, at], o_hbm.at[:, at], out_sem.at[i])

    for i in range(tiles):
        out[:, i * tile:(i + 1) * tile] = jnp.dot(
            att[...], wout[:, i * tile:(i + 1) * tile], preferred_element_type=jnp.float32
        ).astype(jnp.bfloat16)
        store(i).start()
    for i in range(len(sends)):
        @pl.when(sends[i][2])
        def _(i=i):
            for k in range(PARTS):
                remote(i, k).wait_send()
    for i in range(tiles):
        store(i).wait()


def local(n, queries, latent_rope, doc_start, w_kv_up, w_out):
    rows = queries.shape[0]
    heads = w_out.shape[0] // DV
    part = rows // PARTS
    sends = 11
    bf, f32 = jnp.bfloat16, jnp.float32
    return pl.pallas_call(
        functools.partial(kernel, n, heads),
        out_shape=jax.ShapeDtypeStruct((rows, w_out.shape[1]), bf),
        in_specs=[pl.BlockSpec(memory_space=pltpu.HBM)] * 5,
        out_specs=pl.BlockSpec(memory_space=pltpu.HBM),
        scratch_shapes=[
            pltpu.VMEM((REACH + 1, PARTS, R + DR, part), bf),
            pltpu.VMEM(queries.shape, bf),
            pltpu.VMEM((heads, DQ, rows), bf),
            pltpu.VMEM(doc_start.shape, jnp.int32),
            pltpu.VMEM((R, heads * DN), bf),
            pltpu.VMEM((R, heads * DV), bf),
            pltpu.VMEM((heads * DV, R), bf),
            pltpu.VMEM(w_out.shape, bf),
            pltpu.VMEM(latent_rope.shape, bf),
            pltpu.VMEM((rows, rows), f32),
            pltpu.VMEM((heads, DV + 16, rows), f32),
            pltpu.VMEM((heads, 1, rows), f32),
            pltpu.VMEM((rows, heads * DV), bf),
            pltpu.VMEM((rows, w_out.shape[1]), bf),
            pltpu.SemaphoreType.DMA((PARTS,)),
            pltpu.SemaphoreType.DMA((3,)),
            pltpu.SemaphoreType.DMA((2, heads)),
            pltpu.SemaphoreType.DMA((4,)),
            pltpu.SemaphoreType.DMA((sends, PARTS)),
            pltpu.SemaphoreType.DMA((REACH + 1, PARTS)),
        ],
        compiler_params=pltpu.CompilerParams(
            collective_id=0, has_side_effects=True, vmem_limit_bytes=60 * 1024 * 1024
        ),
        cost_estimate=pl.CostEstimate(
            flops=20 * 10**9, bytes_accessed=10**7, transcendentals=8 * heads * rows * rows
        ),
    )(queries, latent_rope.T, doc_start, w_kv_up, w_out)


def solution(mesh):
    in_specs = (P(("grp", "srv"), None), P(("grp", "srv"), None), P(("grp", "srv")), P(), P())
    out_specs = P(("grp", "srv"), None)
    return jax.shard_map(
        functools.partial(local, mesh.shape["srv"]), mesh=mesh, in_specs=in_specs, out_specs=out_specs,
        check_vma=False,
    )
```

```python
import functools
import math

import jax
import jax.numpy as jnp
from jax import lax
from jax.experimental import pallas as pl
from jax.experimental.pallas import tpu as pltpu
from jax.sharding import PartitionSpec as P

DN = 128
DR = 64
DV = 128
R = 512
REACH = 7
DQ = DN + DR
PARTS = 3
NEG = -1e30
MESH = pl.DeviceIdType.MESH

ORDER = ((4, 2, 3, 6, 1, 7, 5), (1, 5, 4, 3, 2, 7, 6), (2, 4, 1, 3, 6, 7, 5), (1, 3, 2, 4, 5, 7, 6))
TAKE = (
    ((4,), (2,), (3,), (6,), (1,), (7, 5), ()),
    ((1,), (5,), (4,), (3,), (2,), (7,), (6,)),
    ((2, 4), (), (1, 6), (3, 7), (), (), (5,)),
    ((1,), (3, 2, 4), (), (), (5, 6), (7,), ()),
)


def kernel(n, heads, q_hbm, lat_hbm, start_hbm, wkv_hbm, o_hbm,
           held, q_in, q_s, start_in, wk, wv, wvt, lat, bias, acc, top, att,
           lat_sem, in_sem, w_sem, out_sem, send_sem, recv_sem):
    rows = q_in.shape[0]
    part = rows // PARTS
    me = lax.axis_index("srv")
    z, x, c = me // 4, (me // 2) % 2, me % 2
    depth = n // 4
    place = 2 * x + c
    scale = math.log2(math.e) / math.sqrt(DQ)

    own_loads = [
        pltpu.make_async_copy(lat_hbm.at[:, pl.ds(k * part, part)], held.at[0, k], lat_sem.at[k])
        for k in range(PARTS)
    ]
    loads = [
        pltpu.make_async_copy(a, b, in_sem.at[i])
        for i, (a, b) in enumerate(((start_hbm, start_in), (q_hbm, q_in)))
    ]
    w_loads = [
        pltpu.make_async_copy(
            wkv_hbm.at[:, pl.ds(h * (DN + DV) + i * DN, DN)], b.at[:, pl.ds(h * DN, DN)], w_sem.at[i, h]
        )
        for i, b in ((0, wk), (1, wv))
        for h in range(heads)
    ]
    for load in own_loads + loads + w_loads:
        load.start()

    has_next = z + 1 < depth
    middle = jnp.logical_and(z >= 1, has_next)
    partners = (
        (1 - 2 * c, True),
        (2 - 4 * x, True),
        (4, has_next),
        (-4, z >= 1),
        (3, jnp.logical_and(c == 1, middle)),
        (-3, jnp.logical_and(c == 0, z >= 2)),
    )
    barrier = pltpu.get_barrier_semaphore()
    for delta, cond in partners:
        def greet(delta=delta):
            pl.semaphore_signal(barrier, inc=1, device_id={"srv": me + delta}, device_id_type=MESH)
        greet() if cond is True else pl.when(cond)(greet)

    corner = jnp.logical_and(x == 0, c == 0)
    sends = (
        (0, 1, c == 0),
        (0, 2, x == 0),
        (0, 4, has_next),
        (2, 1 - 2 * c, me >= 2),
        (2, 4, jnp.logical_and(corner, middle)),
        (4, 1 - 2 * c, z >= 1),
        (4, 2 - 4 * x, z >= 1),
        (4, 3, jnp.logical_and(c == 1, middle)),
        (5, 1, jnp.logical_and(corner, z >= 2)),
        (6, 1 - 2 * c, jnp.logical_and(me >= 6, jnp.logical_or(x == 1, c == 0))),
        (7, -2, jnp.logical_and(jnp.logical_and(x == 1, c == 0), me >= 7)),
    )

    def remote(i, k):
        d, delta, _ = sends[i]
        return pltpu.make_async_remote_copy(
            src_ref=held.at[d, k],
            dst_ref=held.at[d + delta, k],
            send_sem=send_sem.at[i, k],
            recv_sem=recv_sem.at[d + delta, k],
            device_id={"srv": me + delta},
            device_id_type=MESH,
        )

    def pass_on(d, k):
        for i, (source, _, cond) in enumerate(sends):
            if source == d:
                pl.when(cond)(lambda i=i: remote(i, k).start())

    def take(distances):
        for k in range(PARTS):
            for d in distances:
                @pl.when(d <= me)
                def _(d=d):
                    pltpu.make_async_remote_copy(
                        src_ref=held.at[d, k],
                        dst_ref=held.at[d, k],
                        send_sem=send_sem.at[0, k],
                        recv_sem=recv_sem.at[d, k],
                        device_id={"srv": me + 1 - 2 * c},
                        device_id_type=MESH,
                    ).wait_recv()
                    pass_on(d, k)

    count = 2 + has_next.astype(jnp.int32) + (z >= 1).astype(jnp.int32)
    count = count + jnp.logical_and(c == 1, middle).astype(jnp.int32)
    count = count + jnp.logical_and(c == 0, z >= 2).astype(jnp.int32)

    for load in own_loads:
        load.wait()
    pl.semaphore_wait(barrier, count)
    @pl.when(c == 0)
    def _():
        for k in range(PARTS):
            pass_on(0, k)

    loads[1].wait()
    for h in range(heads):
        q_s[h] = jnp.transpose(q_in[:, h * DQ:(h + 1) * DQ])
    for load in w_loads:
        load.wait()
    for h in range(heads):
        wvt[h * DV:(h + 1) * DV, :] = jnp.transpose(wv[:, h * DV:(h + 1) * DV])
    loads[0].wait()

    def block(d, own):
        for k in range(PARTS):
            lat[k * part:(k + 1) * part, :] = jnp.transpose(held[d, k])
        first = start_in[...].reshape(1, rows) - (me - d) * rows
        position = lax.broadcasted_iota(jnp.int32, (rows, rows), 0)
        allowed = position >= first
        if own:
            allowed = jnp.logical_and(allowed, position <= lax.broadcasted_iota(jnp.int32, (rows, rows), 1))
        bias[...] = jnp.where(allowed, jnp.float32(0.0), jnp.float32(NEG))
        ones = jnp.ones((16, rows), jnp.bfloat16)

        latent_t = jnp.concatenate([held[d, k, :R, :] for k in range(PARTS)], axis=1)

        def expand(pair):
            at = slice(pair * 2 * DN, (pair + 1) * 2 * DN)
            k_nope = jnp.dot(lat[:, :R], wk[:, at], preferred_element_type=jnp.float32)
            values = jnp.dot(wvt[at, :], latent_t, preferred_element_type=jnp.float32)
            return k_nope.astype(jnp.bfloat16), values.astype(jnp.bfloat16)

        def score(h, pair):
            i = h % 2
            keys = jnp.concatenate([pair[0][:, i * DN:(i + 1) * DN], lat[:, R:]], axis=1)
            return jnp.dot(keys, q_s[h], preferred_element_type=jnp.float32)

        def weigh(h, s):
            s = s + bias[...]
            new = jnp.max(s, axis=0, keepdims=True)
            factor = None
            if not own:
                old = top[h]
                new = jnp.maximum(old, new)
                factor = jnp.exp2((old - new) * scale)
            top[h] = new
            return jnp.exp2((s - new) * scale).astype(jnp.bfloat16), factor

        def add(h, pair, p, factor):
            i = h % 2
            values = jnp.concatenate([pair[1][i * DV:(i + 1) * DV, :], ones], axis=0)
            pv = jnp.dot(values, p, preferred_element_type=jnp.float32)
            acc[h] = pv if own else acc[h] * factor + pv

        pairs = {0: expand(0)}
        scores = {0: score(0, pairs[0])}
        for h in range(heads):
            if h + 1 < heads:
                scores[h + 1] = score(h + 1, pairs[(h + 1) // 2])
            if h % 2 == 0 and h + 2 < heads:
                pairs[h // 2 + 1] = expand(h // 2 + 1)
            add(h, pairs[h // 2], *weigh(h, scores.pop(h)))

    block(0, True)

    @pl.when(c == 1)
    def _():
        for k in range(PARTS):
            pass_on(0, k)

    def digits(order):
        return sum(d * 8**i for i, d in enumerate(order))

    codes = [digits(order) for order in ORDER]
    code = (
        (1 - x) * (1 - c) * codes[0] + (1 - x) * c * codes[1] + x * (1 - c) * codes[2] + x * c * codes[3]
    )

    def step(t, code):
        for i in range(REACH):
            for p in range(4):
                if TAKE[p][i]:
                    @pl.when(jnp.logical_and(t == i, place == p))
                    def _(p=p, i=i):
                        take(TAKE[p][i])
        d = code % 8
        pl.when(d <= me)(lambda: block(d, False))
        return code // 8

    lax.fori_loop(0, REACH, step, code)

    for h in range(heads):
        attended = acc[h, :DV, :] / acc[h, DV:DV + 1, :]
        att[:, h * DV:(h + 1) * DV] = jnp.transpose(attended.astype(jnp.bfloat16))
    store = pltpu.make_async_copy(att, o_hbm, out_sem)
    store.start()
    for i in range(len(sends)):
        @pl.when(sends[i][2])
        def _(i=i):
            for k in range(PARTS):
                remote(i, k).wait_send()
    store.wait()


def local(n, queries, latent_rope, doc_start, w_kv_up, w_out):
    rows = queries.shape[0]
    heads = w_out.shape[0] // DV
    part = rows // PARTS
    sends = 11
    bf, f32 = jnp.bfloat16, jnp.float32
    attended = pl.pallas_call(
        functools.partial(kernel, n, heads),
        out_shape=jax.ShapeDtypeStruct((rows, heads * DV), bf),
        in_specs=[pl.BlockSpec(memory_space=pltpu.HBM)] * 4,
        out_specs=pl.BlockSpec(memory_space=pltpu.HBM),
        scratch_shapes=[
            pltpu.VMEM((REACH + 1, PARTS, R + DR, part), bf),
            pltpu.VMEM(queries.shape, bf),
            pltpu.VMEM((heads, DQ, rows), bf),
            pltpu.VMEM(doc_start.shape, jnp.int32),
            pltpu.VMEM((R, heads * DN), bf),
            pltpu.VMEM((R, heads * DV), bf),
            pltpu.VMEM((heads * DV, R), bf),
            pltpu.VMEM(latent_rope.shape, bf),
            pltpu.VMEM((rows, rows), f32),
            pltpu.VMEM((heads, DV + 16, rows), f32),
            pltpu.VMEM((heads, 1, rows), f32),
            pltpu.VMEM((rows, heads * DV), bf),
            pltpu.SemaphoreType.DMA((PARTS,)),
            pltpu.SemaphoreType.DMA((2,)),
            pltpu.SemaphoreType.DMA((2, heads)),
            pltpu.SemaphoreType.DMA,
            pltpu.SemaphoreType.DMA((sends, PARTS)),
            pltpu.SemaphoreType.DMA((REACH + 1, PARTS)),
        ],
        compiler_params=pltpu.CompilerParams(
            collective_id=0, has_side_effects=True, vmem_limit_bytes=60 * 1024 * 1024
        ),
        cost_estimate=pl.CostEstimate(
            flops=20 * 10**9, bytes_accessed=10**7, transcendentals=8 * heads * rows * rows
        ),
    )(queries, latent_rope.T, doc_start, w_kv_up)
    return jnp.dot(attended, w_out, preferred_element_type=f32).astype(bf)


def solution(mesh):
    in_specs = (P(("grp", "srv"), None), P(("grp", "srv"), None), P(("grp", "srv")), P(), P())
    out_specs = P(("grp", "srv"), None)
    return jax.shard_map(
        functools.partial(local, mesh.shape["srv"]), mesh=mesh, in_specs=in_specs, out_specs=out_specs,
        check_vma=False,
    )
```

```python
import functools
import math

import jax
import jax.numpy as jnp
from jax import lax
from jax.experimental import pallas as pl
from jax.experimental.pallas import tpu as pltpu
from jax.sharding import PartitionSpec as P

DN = 128
DR = 64
DV = 128
R = 512
REACH = 7
DQ = DN + DR
PARTS = 3
NEG = -1e30
MESH = pl.DeviceIdType.MESH

ORDER = ((4, 2, 3, 6, 1, 7, 5), (1, 5, 3, 4, 2, 7, 6), (2, 4, 1, 6, 3, 7, 5), (1, 3, 2, 4, 5, 7, 6))
TAKE = (
    ((4,), (2,), (3,), (6,), (1,), (7, 5), ()),
    ((1,), (5,), (3, 4), (2,), (), (7,), (6,)),
    ((2, 4), (), (1, 6), (3,), (7,), (), (5,)),
    ((1,), (3, 2), (4,), (5,), (6,), (7,), ()),
)


def kernel(n, heads, q_hbm, lat_hbm, start_hbm, wkv_hbm, wout_hbm, o_hbm,
           held, q_in, q_s, start_in, wk, wv, wvt, wout, lat, bias, acc, top, att, out,
           lat_sem, in_sem, w_sem, out_sem, send_sem, recv_sem):
    rows = q_in.shape[0]
    part = rows // PARTS
    me = lax.axis_index("srv")
    z, x, c = me // 4, (me // 2) % 2, me % 2
    depth = n // 4
    place = 2 * x + c
    scale = math.log2(math.e) / math.sqrt(DQ)

    own_loads = [
        pltpu.make_async_copy(lat_hbm.at[:, pl.ds(k * part, part)], held.at[0, k], lat_sem.at[k])
        for k in range(PARTS)
    ]
    loads = [
        pltpu.make_async_copy(a, b, in_sem.at[i])
        for i, (a, b) in enumerate(((start_hbm, start_in), (q_hbm, q_in), (wout_hbm, wout)))
    ]
    w_loads = [
        pltpu.make_async_copy(
            wkv_hbm.at[:, pl.ds(h * (DN + DV) + i * DN, DN)], b.at[:, pl.ds(h * DN, DN)], w_sem.at[i, h]
        )
        for i, b in ((0, wk), (1, wv))
        for h in range(heads)
    ]
    for load in own_loads + loads[:2] + w_loads + loads[2:]:
        load.start()

    has_next = z + 1 < depth
    middle = jnp.logical_and(z >= 1, has_next)
    partners = (
        (1 - 2 * c, True),
        (2 - 4 * x, True),
        (4, has_next),
        (-4, z >= 1),
        (3, jnp.logical_and(c == 1, middle)),
        (-3, jnp.logical_and(c == 0, z >= 2)),
    )
    barrier = pltpu.get_barrier_semaphore()
    for delta, cond in partners:
        def greet(delta=delta):
            pl.semaphore_signal(barrier, inc=1, device_id={"srv": me + delta}, device_id_type=MESH)
        greet() if cond is True else pl.when(cond)(greet)

    corner = jnp.logical_and(x == 0, c == 0)
    sends = (
        (0, 1, c == 0),
        (0, 2, x == 0),
        (0, 4, has_next),
        (2, 1 - 2 * c, me >= 2),
        (2, 4, jnp.logical_and(corner, middle)),
        (4, 1 - 2 * c, z >= 1),
        (4, 2 - 4 * x, z >= 1),
        (4, 3, jnp.logical_and(c == 1, middle)),
        (5, 1, jnp.logical_and(corner, z >= 2)),
        (6, 1 - 2 * c, jnp.logical_and(me >= 6, jnp.logical_or(x == 1, c == 0))),
        (7, -2, jnp.logical_and(jnp.logical_and(x == 1, c == 0), me >= 7)),
    )

    def remote(i, k):
        d, delta, _ = sends[i]
        return pltpu.make_async_remote_copy(
            src_ref=held.at[d, k],
            dst_ref=held.at[d + delta, k],
            send_sem=send_sem.at[i, k],
            recv_sem=recv_sem.at[d + delta, k],
            device_id={"srv": me + delta},
            device_id_type=MESH,
        )

    def pass_on(d, k):
        for i, (source, _, cond) in enumerate(sends):
            if source == d:
                pl.when(cond)(lambda i=i: remote(i, k).start())

    def take(distances):
        for k in range(PARTS):
            for d in distances:
                @pl.when(d <= me)
                def _(d=d):
                    pltpu.make_async_remote_copy(
                        src_ref=held.at[d, k],
                        dst_ref=held.at[d, k],
                        send_sem=send_sem.at[0, k],
                        recv_sem=recv_sem.at[d, k],
                        device_id={"srv": me + 1 - 2 * c},
                        device_id_type=MESH,
                    ).wait_recv()
                    pass_on(d, k)

    count = 2 + has_next.astype(jnp.int32) + (z >= 1).astype(jnp.int32)
    count = count + jnp.logical_and(c == 1, middle).astype(jnp.int32)
    count = count + jnp.logical_and(c == 0, z >= 2).astype(jnp.int32)

    for load in own_loads:
        load.wait()
    pl.semaphore_wait(barrier, count)
    @pl.when(c == 0)
    def _():
        for k in range(PARTS):
            pass_on(0, k)

    loads[1].wait()
    for h in range(heads):
        q_s[h] = jnp.transpose(q_in[:, h * DQ:(h + 1) * DQ])
    for load in w_loads:
        load.wait()
    for h in range(heads):
        wvt[h * DV:(h + 1) * DV, :] = jnp.transpose(wv[:, h * DV:(h + 1) * DV])
    loads[0].wait()

    def block(d, own):
        for k in range(PARTS):
            lat[k * part:(k + 1) * part, :] = jnp.transpose(held[d, k])
        first = start_in[...].reshape(1, rows) - (me - d) * rows
        position = lax.broadcasted_iota(jnp.int32, (rows, rows), 0)
        allowed = position >= first
        if own:
            allowed = jnp.logical_and(allowed, position <= lax.broadcasted_iota(jnp.int32, (rows, rows), 1))
        bias[...] = jnp.where(allowed, jnp.float32(0.0), jnp.float32(NEG))
        ones = jnp.ones((16, rows), jnp.bfloat16)

        latent_t = jnp.concatenate([held[d, k, :R, :] for k in range(PARTS)], axis=1)

        def expand(pair):
            at = slice(pair * 2 * DN, (pair + 1) * 2 * DN)
            k_nope = jnp.dot(lat[:, :R], wk[:, at], preferred_element_type=jnp.float32)
            values = jnp.dot(wvt[at, :], latent_t, preferred_element_type=jnp.float32)
            return k_nope.astype(jnp.bfloat16), values.astype(jnp.bfloat16)

        def score(h, pair):
            i = h % 2
            keys = jnp.concatenate([pair[0][:, i * DN:(i + 1) * DN], lat[:, R:]], axis=1)
            return jnp.dot(keys, q_s[h], preferred_element_type=jnp.float32)

        def weigh(h, s):
            s = s + bias[...]
            new = jnp.max(s, axis=0, keepdims=True)
            factor = None
            if not own:
                old = top[h]
                new = jnp.maximum(old, new)
                factor = jnp.exp2((old - new) * scale)
            top[h] = new
            return jnp.exp2((s - new) * scale).astype(jnp.bfloat16), factor

        def add(h, pair, p, factor):
            i = h % 2
            values = jnp.concatenate([pair[1][i * DV:(i + 1) * DV, :], ones], axis=0)
            pv = jnp.dot(values, p, preferred_element_type=jnp.float32)
            acc[h] = pv if own else acc[h] * factor + pv

        pairs = {0: expand(0)}
        scores = {0: score(0, pairs[0])}
        for h in range(heads):
            if h + 1 < heads:
                scores[h + 1] = score(h + 1, pairs[(h + 1) // 2])
            if h % 2 == 0 and h + 2 < heads:
                pairs[h // 2 + 1] = expand(h // 2 + 1)
            add(h, pairs[h // 2], *weigh(h, scores.pop(h)))

    block(0, True)

    @pl.when(c == 1)
    def _():
        for k in range(PARTS):
            pass_on(0, k)

    def digits(order):
        return sum(d * 8**i for i, d in enumerate(order))

    codes = [digits(order) for order in ORDER]
    code = (
        (1 - x) * (1 - c) * codes[0] + (1 - x) * c * codes[1] + x * (1 - c) * codes[2] + x * c * codes[3]
    )

    def step(t, code):
        for i in range(REACH):
            for p in range(4):
                if TAKE[p][i]:
                    @pl.when(jnp.logical_and(t == i, place == p))
                    def _(p=p, i=i):
                        take(TAKE[p][i])
        d = code % 8
        pl.when(d <= me)(lambda: block(d, False))
        return code // 8

    lax.fori_loop(0, REACH, step, code)

    for h in range(heads):
        attended = acc[h, :DV, :] / acc[h, DV:DV + 1, :]
        att[:, h * DV:(h + 1) * DV] = jnp.transpose(attended.astype(jnp.bfloat16))
    loads[2].wait()
    width = wout.shape[1]
    tile = 512
    tiles = width // tile

    def store(i):
        at = pl.ds(i * tile, tile)
        return pltpu.make_async_copy(out.at[:, at], o_hbm.at[:, at], out_sem.at[i])

    for i in range(tiles):
        out[:, i * tile:(i + 1) * tile] = jnp.dot(
            att[...], wout[:, i * tile:(i + 1) * tile], preferred_element_type=jnp.float32
        ).astype(jnp.bfloat16)
        store(i).start()
    for i in range(len(sends)):
        @pl.when(sends[i][2])
        def _(i=i):
            for k in range(PARTS):
                remote(i, k).wait_send()
    for i in range(tiles):
        store(i).wait()


def local(n, queries, latent_rope, doc_start, w_kv_up, w_out):
    rows = queries.shape[0]
    heads = w_out.shape[0] // DV
    part = rows // PARTS
    sends = 11
    bf, f32 = jnp.bfloat16, jnp.float32
    return pl.pallas_call(
        functools.partial(kernel, n, heads),
        out_shape=jax.ShapeDtypeStruct((rows, w_out.shape[1]), bf),
        in_specs=[pl.BlockSpec(memory_space=pltpu.HBM)] * 5,
        out_specs=pl.BlockSpec(memory_space=pltpu.HBM),
        scratch_shapes=[
            pltpu.VMEM((REACH + 1, PARTS, R + DR, part), bf),
            pltpu.VMEM(queries.shape, bf),
            pltpu.VMEM((heads, DQ, rows), bf),
            pltpu.VMEM(doc_start.shape, jnp.int32),
            pltpu.VMEM((R, heads * DN), bf),
            pltpu.VMEM((R, heads * DV), bf),
            pltpu.VMEM((heads * DV, R), bf),
            pltpu.VMEM(w_out.shape, bf),
            pltpu.VMEM(latent_rope.shape, bf),
            pltpu.VMEM((rows, rows), f32),
            pltpu.VMEM((heads, DV + 16, rows), f32),
            pltpu.VMEM((heads, 1, rows), f32),
            pltpu.VMEM((rows, heads * DV), bf),
            pltpu.VMEM((rows, w_out.shape[1]), bf),
            pltpu.SemaphoreType.DMA((PARTS,)),
            pltpu.SemaphoreType.DMA((3,)),
            pltpu.SemaphoreType.DMA((2, heads)),
            pltpu.SemaphoreType.DMA((4,)),
            pltpu.SemaphoreType.DMA((sends, PARTS)),
            pltpu.SemaphoreType.DMA((REACH + 1, PARTS)),
        ],
        compiler_params=pltpu.CompilerParams(
            collective_id=0, has_side_effects=True, vmem_limit_bytes=58 * 1024 * 1024
        ),
        cost_estimate=pl.CostEstimate(
            flops=20 * 10**9, bytes_accessed=10**7, transcendentals=8 * heads * rows * rows
        ),
    )(queries, latent_rope.T, doc_start, w_kv_up, w_out)


def solution(mesh):
    in_specs = (P(("grp", "srv"), None), P(("grp", "srv"), None), P(("grp", "srv")), P(), P())
    out_specs = P(("grp", "srv"), None)
    return jax.shard_map(
        functools.partial(local, mesh.shape["srv"]), mesh=mesh, in_specs=in_specs, out_specs=out_specs,
        check_vma=False,
    )
```
